32 devices in a mesh: grp: 2 (over x), fsdp: 16 (over z, y, core).
Axes of the slice: x: 2, y: 2, z: 4, core: 2. Of those that a mesh axis runs over, the one named last changes fastest.
Arguments:
- latent: bfloat16 [512, 6144], P('grp'), parts along dimension 0, may hold values from -400 to 400
- adjoint: bfloat16 [512, 6144], P(('grp', 'fsdp')), parts along dimension 0, may hold values from -6 to 6
- shift_row: float32 [12288], P('grp'), parts along dimension 0, may hold values from -4 to 4
- scale_row: float32 [12288], P('grp'), parts along dimension 0, may hold values from -2.5 to 2.5
- gate_row: float32 [12288], P('grp'), parts along dimension 0, may hold values from -4 to 4
- b_up: bfloat16 [24576], P('fsdp'), may hold values from -3 to 3
- w_up: bfloat16 [6144, 24576], P(None, 'fsdp'), may hold values from -0.078125 to 0.078125
- w_down: bfloat16 [24576, 6144], P('fsdp'), may hold values from -0.0390625 to 0.0390625
Outputs:
- new_adjoint: float32 [512, 6144], P(('grp', 'fsdp')), parts along dimension 0
The draws below stay inside these ranges and needn't reach their ends.
There are 2 independent parts, one for each index of `grp`. The reference program is written for one: setup_inputs(seed, part) draws one part's arguments, and reference() takes and returns one part's arrays. A program takes and returns all parts, laid end to end along the dimension named above; an argument that names none is the same for every part. Nothing has to cross between parts.
All inputs are finite; a program needn't handle non-finite values.
Results may differ from the reference program's by a relative error of at most 0.00064.
Values may be sent and summed in bfloat16 or wider, within the bound.
No kernel may reach another device: no remote copies, remote signals or barrier semaphores. Data moves between devices by JAX's collectives and lax.ppermute only.
A program may use at most 128 MiB of HBM per device.

```python
import math
import jax
import jax.numpy as jnp
from jax import lax

D = 6144
FF = 24576
TOKENS = 256


def draw_latent(key, part):
    key = jax.random.fold_in(key, 11)
    k_base, k_rows, k_cols = jax.random.split(key, 3)
    base = jax.random.normal(k_base, (TOKENS, D), jnp.float32)
    row_scale = jnp.exp(jax.random.uniform(k_rows, (TOKENS, 1), jnp.float32, 0.0, math.log(10.0)))
    col_scale = jnp.exp(jax.random.uniform(k_cols, (1, D), jnp.float32, math.log(0.3), math.log(3.0)))
    values = base * col_scale * row_scale
    return jnp.clip(values, -400.0, 400.0).astype(jnp.bfloat16)


def level_of(own_key, extent, cuts, smallest, top_value):
    factor_of = 1.0
    for axis_at, shards_of in cuts:
        heights = jax.random.uniform(jax.random.fold_in(jax.random.fold_in(own_key, 6), axis_at), (shards_of,), jnp.float32, smallest / len(cuts), top_value / len(cuts))
        factor_of = factor_of * jnp.repeat(jnp.exp(heights), extent[axis_at] // shards_of).reshape((-1,) + (1,) * (len(extent) - 1 - axis_at))
    return factor_of


def scatter_about(rng, shape, width, reach, pieces=(), held_as=jnp.bfloat16):
    level = level_of(rng, shape, pieces, -0.22, 0.18) if pieces else 1.0
    entries = jax.random.normal(rng, shape, jnp.float32) * width * level
    return jnp.minimum(jnp.maximum(entries, -reach), reach).astype(held_as)


def setup_inputs(seed: int = 0, part: int = 0) -> dict:
    seeds = jax.random.split(jax.random.key(seed), 9)
    part_splits = jax.random.split(jax.random.fold_in(seeds[8], part), 9)
    return {
        "latent": draw_latent(jax.random.fold_in(jax.random.fold_in(seeds[8], part), 71), part),
        "adjoint": scatter_about(part_splits[1], (TOKENS, D), 1.0, 6.0, ((0, 16),)),
        "shift_row": scatter_about(part_splits[2], (D,), 1.0, 4.0, (), jnp.float32),
        "scale_row": scatter_about(part_splits[3], (D,), 0.5, 2.5, (), jnp.float32),
        "gate_row": scatter_about(part_splits[4], (D,), 1.0, 4.0, (), jnp.float32),
        "b_up": scatter_about(seeds[5], (FF,), 0.5, 3.0, ((0, 16),)),
        "w_up": scatter_about(seeds[6], (D, FF), D ** -0.5, 0.078125, ((1, 16),)),
        "w_down": scatter_about(seeds[7], (FF, D), FF ** -0.5, 0.0390625, ((0, 16),)),
    }


step_scale = 0.5

def gelu_slope(u):
    k = 0.7978845608
    t = jnp.tanh(k * (u + 0.044715 * u * u * u))
    return 0.5 * (1.0 + t) + 0.5 * u * (1.0 - t * t) * k * (1.0 + 3.0 * 0.044715 * u * u)

def normalize(latent):
    values = latent.astype(jnp.float32)
    mean = lax.optimization_barrier(jnp.mean(values, axis=1, keepdims=True))
    centred = values - mean
    rstd = lax.rsqrt(lax.optimization_barrier(jnp.mean(centred * centred, axis=1, keepdims=True)) + 1e-06)
    return (centred * rstd, rstd)

def norm_back(dh_rows, normed, rstd, scale):
    scaled = (1.0 + scale) * dh_rows
    first = lax.optimization_barrier(jnp.mean(scaled, axis=1, keepdims=True))
    second = lax.optimization_barrier(jnp.mean(scaled * normed, axis=1, keepdims=True))
    return rstd * (scaled - first - normed * second)

def reference(latent, adjoint, shift_row, scale_row, gate_row, b_up, w_up, w_down):
    normed, rstd = normalize(latent)
    hidden_in = (normed * (1.0 + scale_row) + shift_row).astype(jnp.bfloat16)
    gated = (gate_row * adjoint.astype(jnp.float32)).astype(jnp.bfloat16)
    upper = jnp.dot(hidden_in, w_up, preferred_element_type=jnp.float32) + b_up.astype(jnp.float32)
    d_act = lax.dot_general(gated, w_down, (((1,), (1,)), ((), ())), preferred_element_type=jnp.float32)
    d_upper = (d_act * gelu_slope(upper)).astype(jnp.bfloat16)
    d_hidden = lax.dot_general(d_upper, w_up, (((1,), (1,)), ((), ())), preferred_element_type=jnp.float32)
    d_latent = norm_back(d_hidden, normed, rstd, scale_row)
    return adjoint.astype(jnp.float32) + step_scale * d_latent
```

```python
import jax
import jax.numpy as jnp
from jax import lax
from jax.sharding import PartitionSpec as P

step_scale = 0.5


def gelu_slope(u):
    k = 0.7978845608
    t = jnp.tanh(k * (u + 0.044715 * u * u * u))
    return 0.5 * (1.0 + t) + 0.5 * u * (1.0 - t * t) * k * (1.0 + 3.0 * 0.044715 * u * u)


def normalize(latent):
    values = latent.astype(jnp.float32)
    mean = jnp.mean(values, axis=1, keepdims=True)
    centred = values - mean
    rstd = lax.rsqrt(jnp.mean(centred * centred, axis=1, keepdims=True) + 1e-06)
    return (centred * rstd, rstd)


def finish(latent_rows, adjoint, scale_row, d_hidden):
    normed, rstd = normalize(latent_rows)
    scaled = (1.0 + scale_row) * d_hidden
    first = jnp.mean(scaled, axis=1, keepdims=True)
    second = jnp.mean(scaled * normed, axis=1, keepdims=True)
    d_latent = rstd * (scaled - first - normed * second)
    return adjoint.astype(jnp.float32) + step_scale * d_latent


def rows_t(a, b):
    return lax.dot_general(a, b, (((1,), (1,)), ((), ())), preferred_element_type=jnp.float32)


def general(latent, adjoint, shift_row, scale_row, gate_row, b_up, w_up, w_down):
    own_rows = adjoint.shape[0]
    start = lax.axis_index("fsdp") * own_rows
    normed, _ = normalize(latent)
    hidden_in = (normed * (1.0 + scale_row) + shift_row).astype(jnp.bfloat16)
    gated = (gate_row * adjoint.astype(jnp.float32)).astype(jnp.bfloat16)
    gated = lax.all_gather(gated, "fsdp", axis=0, tiled=True)
    upper = jnp.dot(hidden_in, w_up, preferred_element_type=jnp.float32) + b_up.astype(jnp.float32)
    d_upper = (rows_t(gated, w_down) * gelu_slope(upper)).astype(jnp.bfloat16)
    d_hidden = lax.psum_scatter(rows_t(d_upper, w_up), "fsdp", scatter_dimension=0, tiled=True)
    return finish(lax.dynamic_slice_in_dim(latent, start, own_rows, 0), adjoint, scale_row, d_hidden)


def middle(i):
    return (i >> 2) in (1, 2)


CORE = [(i, i ^ 1) for i in range(16)]
SIDE = [(i, i ^ 2) for i in range(16)]
SIDE_ENDS = [(i, i ^ 2) for i in range(16) if not middle(i)]
PAIR = [(i, i ^ 4) for i in range(16)]
PAIR_OUT = [(i, i ^ 4) for i in range(16) if middle(i)]
PAIR_IN = [(i, i ^ 4) for i in range(16) if not middle(i)]
MID = [(i, i ^ 12) for i in range(16) if middle(i)]


def send(x, pairs):
    return lax.ppermute(x, "fsdp", pairs)


def gather_rows(own, is_mid):
    b00 = own
    b01 = send(b00, SIDE)
    b10 = send(b00, PAIR)
    m1 = send(b00, MID)
    m2 = send(b10, MID)
    a2 = send(jnp.where(is_mid, m1, b01), PAIR)
    y2 = send(jnp.where(is_mid, m1, b10), SIDE)
    b20 = jnp.where(is_mid, m2, a2)
    b11 = jnp.where(is_mid, a2, y2)
    a3 = send(m2, PAIR_OUT)
    b21 = send(b20, SIDE)
    y4 = send(a3, SIDE_ENDS)
    b30 = jnp.where(is_mid, m1, a3)
    b31 = jnp.where(is_mid, y2, y4)
    return [b00, b01, b10, b11, b20, b21, b30, b31]


def scatter_sums(p, is_mid):
    half = lambda x: x.astype(jnp.float16)
    wide = lambda x: x.astype(jnp.float32)
    p00, p01, p10, p11, p20, p21, p30, p31 = p
    y4 = wide(send(half(p31), SIDE_ENDS))
    y3 = wide(send(half(p21), SIDE))
    a3 = wide(send(half(p30 + y4), PAIR_IN))
    y2 = wide(send(half(jnp.where(is_mid, p31, p11)), SIDE))
    p20 = p20 + y3 + a3
    a2 = wide(send(half(jnp.where(is_mid, p11, p20)), PAIR))
    m2 = wide(send(half(p20), MID))
    p10 = p10 + jnp.where(is_mid, m2, y2)
    p01 = p01 + jnp.where(is_mid, 0.0, a2)
    m1 = wide(send(half(p30 + y2 + a2), MID))
    a1 = wide(send(half(p10), PAIR))
    y1 = wide(send(half(p01), SIDE))
    return p00 + m1 + a1 + y1


def line_of_four(latent, adjoint, shift_row, scale_row, gate_row, b_up, w_up, w_down):
    rows = adjoint.shape[0]
    me = lax.axis_index("fsdp")
    z = me >> 2
    is_mid = (z == 1) | (z == 2)
    order = [dz * 4 + dy * 2 + dc for dc in range(2) for dz in range(4) for dy in range(2)]

    gated = (gate_row * adjoint.astype(jnp.float32)).astype(jnp.bfloat16)
    blocks = gather_rows(gated, is_mid)
    mine = jnp.concatenate(blocks, axis=0)
    gated = jnp.concatenate([mine, send(mine, CORE)], axis=0)

    normed, _ = normalize(latent)
    hidden_in = (normed * (1.0 + scale_row) + shift_row).astype(jnp.bfloat16)
    upper = jnp.dot(hidden_in, w_up, preferred_element_type=jnp.float32) + b_up.astype(jnp.float32)
    slope = gelu_slope(upper)
    slope = jnp.concatenate([lax.dynamic_slice_in_dim(slope, (me ^ k) * rows, rows, 0) for k in order], axis=0)

    unit = 16.0 * jnp.maximum(jnp.max(jnp.abs(gated.astype(jnp.float32)), axis=1, keepdims=True), 1e-30)
    d_upper = (rows_t(gated, w_down) * slope).astype(jnp.bfloat16)
    partial_sum = rows_t(d_upper, w_up) / unit
    n = 8 * rows
    partial_sum = partial_sum[:n] + send(partial_sum[n:].astype(jnp.float16), CORE).astype(jnp.float32)
    d_hidden = scatter_sums([partial_sum[k * rows : (k + 1) * rows] for k in range(8)], is_mid) * unit[:rows]
    return finish(lax.dynamic_slice_in_dim(latent, me * rows, rows, 0), adjoint, scale_row, d_hidden)


def solution(mesh):
    in_specs = (
        P("grp", None),
        P(("grp", "fsdp"), None),
        P("grp"),
        P("grp"),
        P("grp"),
        P("fsdp"),
        P(None, "fsdp"),
        P("fsdp", None),
    )
    out_specs = P(("grp", "fsdp"), None)
    body = line_of_four if mesh.shape["fsdp"] == 16 else general
    return jax.shard_map(body, mesh=mesh, in_specs=in_specs, out_specs=out_specs, check_vma=False)
```

```python
import functools
import jax
import jax.numpy as jnp
from jax import lax
from jax.experimental import pallas as pl
from jax.experimental.pallas import tpu as pltpu
from jax.sharding import PartitionSpec as P

step_scale = 0.5


def gelu_slope(u):
    k = 0.7978845608
    t = jnp.tanh(k * (u + 0.044715 * u * u * u))
    return 0.5 * (1.0 + t) + 0.5 * u * (1.0 - t * t) * k * (1.0 + 3.0 * 0.044715 * u * u)


def normalize(latent):
    values = latent.astype(jnp.float32)
    mean = jnp.mean(values, axis=1, keepdims=True)
    centred = values - mean
    rstd = lax.rsqrt(jnp.mean(centred * centred, axis=1, keepdims=True) + 1e-06)
    return (centred * rstd, rstd)


def finish(latent_rows, adjoint, scale_row, d_hidden):
    normed, rstd = normalize(latent_rows)
    scaled = (1.0 + scale_row) * d_hidden
    first = jnp.mean(scaled, axis=1, keepdims=True)
    second = jnp.mean(scaled * normed, axis=1, keepdims=True)
    d_latent = rstd * (scaled - first - normed * second)
    return adjoint.astype(jnp.float32) + step_scale * d_latent


def rows_t(a, b):
    return lax.dot_general(a, b, (((1,), (1,)), ((), ())), preferred_element_type=jnp.float32)


def general(latent, adjoint, shift_row, scale_row, gate_row, b_up, w_up, w_down):
    own_rows = adjoint.shape[0]
    start = lax.axis_index("fsdp") * own_rows
    normed, _ = normalize(latent)
    hidden_in = (normed * (1.0 + scale_row) + shift_row).astype(jnp.bfloat16)
    gated = (gate_row * adjoint.astype(jnp.float32)).astype(jnp.bfloat16)
    gated = lax.all_gather(gated, "fsdp", axis=0, tiled=True)
    upper = jnp.dot(hidden_in, w_up, preferred_element_type=jnp.float32) + b_up.astype(jnp.float32)
    d_upper = (rows_t(gated, w_down) * gelu_slope(upper)).astype(jnp.bfloat16)
    d_hidden = lax.psum_scatter(rows_t(d_upper, w_up), "fsdp", scatter_dimension=0, tiled=True)
    return finish(lax.dynamic_slice_in_dim(latent, start, own_rows, 0), adjoint, scale_row, d_hidden)


def middle(i):
    return (i >> 2) in (1, 2)


CORE = [(i, i ^ 1) for i in range(16)]
SIDE = [(i, i ^ 2) for i in range(16)]
PAIR = [(i, i ^ 4) for i in range(16)]
CROSS = [(i, i ^ 12) for i in range(16)]
CROSS_MID = [(i, i ^ 12) for i in range(16) if middle(i)]


def send(x, pairs):
    return lax.ppermute(x, "fsdp", pairs)


def half(x):
    return x.astype(jnp.float16)


def wide(x):
    return x.astype(jnp.float32)


def after(x, *done):
    return lax.optimization_barrier((x, *done))[0]


def scatter_sums(quarters, is_mid, rows):
    near_early, near_late, far_early, far_late = quarters
    late = near_late + wide(send(half(far_late), CORE))
    p30, p31, p20, p21 = [late[k * rows : (k + 1) * rows] for k in range(4)]
    y2 = send(half(p21), SIDE)
    early = near_early + wide(send(half(far_early), CORE))
    p00, p01, p10, p11 = [early[k * rows : (k + 1) * rows] for k in range(4)]
    p20 = p20 + wide(y2)
    a2 = send(half(p20), PAIR)
    m2 = send(half(p20), CROSS_MID)
    y3 = send(after(half(p31), y2), SIDE)
    y1 = send(after(half(p11), y3), SIDE)
    p30 = p30 + wide(y3) + jnp.where(is_mid, wide(a2), 0.0)
    x = send(half(p30), CROSS)
    y0 = send(after(half(p01), y1), SIDE)
    a1 = send(half(p10 + wide(y1) + wide(m2)), PAIR)
    return p00 + wide(y0) + wide(x) + wide(a1)


VMEM = pl.BlockSpec(memory_space=pltpu.VMEM)
SMEM = pl.BlockSpec(memory_space=pltpu.SMEM)
HBM = pl.BlockSpec(memory_space=pltpu.HBM)


def kernel(body, specs, out_shape, flops, moved, grant, **more):
    several = isinstance(out_shape, (list, tuple))
    return pl.pallas_call(
        body,
        in_specs=specs,
        out_specs=[VMEM] * len(out_shape) if several else VMEM,
        out_shape=out_shape,
        compiler_params=pltpu.CompilerParams(vmem_limit_bytes=grant * 2**20),
        cost_estimate=pl.CostEstimate(flops=flops, bytes_accessed=moved, transcendentals=0),
        **more,
    )


def load(source, target, sem):
    copy = pltpu.make_async_copy(source, target, sem)
    copy.start()
    return copy


def load_parts(source, start, buf, sems):
    n = buf.shape[1]
    return [load(source.at[pl.ds(start + k * n, n)], buf.at[k], sems.at[k]) for k in range(buf.shape[0])]


def normalize_rows(rows, me_ref, latent_ref, shift_ref, scale_ref, h_ref, own_ref, rstd_ref):
    def block(p):
        g = (p >> 1) & 3
        owner = me_ref[0] ^ ((p >> 3) | ((p & 1) << 1) | ((g ^ (g >> 1)) << 2))
        values = latent_ref[pl.ds(pl.multiple_of(owner * rows, rows), rows), :].astype(jnp.float32)
        mean = jnp.mean(values, axis=1, keepdims=True)
        centred = values - mean
        rstd = lax.rsqrt(jnp.mean(centred * centred, axis=1, keepdims=True) + 1e-06)
        normed = centred * rstd
        h = normed * (1.0 + scale_ref[...]) + shift_ref[...]
        h_ref[pl.ds(pl.multiple_of(p * rows, rows), rows), :] = h.astype(h_ref.dtype)
        return normed, rstd

    own_ref[...], rstd_ref[...] = block(0)

    def step(p, _):
        block(p)
        return 0

    lax.fori_loop(1, 16, step, 0, unroll=3)


def add_products(acc, start, h_ref, copies, w_buf):
    n = w_buf.shape[1]
    for k, copy in enumerate(copies):
        copy.wait()
        product = jnp.dot(h_ref[:, start + k * n : start + (k + 1) * n], w_buf[k], preferred_element_type=jnp.float32)
        acc = product if acc is None else acc + product
    return acc


def first_kernel(rows, me_ref, latent_ref, shift_ref, scale_ref, wu_ref, wd_ref, h_ref, own_ref, rstd_ref, u_ref, wd_out, latent_buf, shift_buf, scale_buf, w_buf, sems, w_sems, wd_sem):
    copies = [
        load(source, target, sems.at[k])
        for k, (source, target) in enumerate([(latent_ref, latent_buf), (shift_ref, shift_buf), (scale_ref, scale_buf)])
    ]
    w_copies = load_parts(wu_ref, 0, w_buf, w_sems)
    wd_copy = load(wd_ref.at[pl.ds(0, wd_out.shape[0])], wd_out, wd_sem)
    for copy in copies:
        copy.wait()
    normalize_rows(rows, me_ref, latent_buf, shift_buf, scale_buf, h_ref, own_ref, rstd_ref)
    u_ref[...] = add_products(None, 0, h_ref, w_copies, w_buf)
    wd_copy.wait()


def second_kernel(start, h_ref, u_ref, wu_ref, u_out, w_buf, w_sems):
    u_out[...] = add_products(u_ref[...], start, h_ref, load_parts(wu_ref, start, w_buf, w_sems), w_buf)


def third_kernel(start, h_ref, u_ref, b_ref, wu_ref, slope_out, w_buf, w_sems):
    second_kernel(start, h_ref, u_ref, wu_ref, slope_out, w_buf, w_sems)
    width = slope_out.shape[1] // 3
    for j in range(3):
        cut = slice(j * width, (j + 1) * width)
        slope_out[:, cut] = gelu_slope(slope_out[:, cut] + b_ref[:, cut].astype(jnp.float32))


def du_kernel(*refs):
    pieces, (wd_early, slope_ref, wd_ref, wu_ref), (du_ref, unit_ref, wu_out, wd_buf, sems) = refs[:6], refs[6:10], refs[10:]
    early, late = wd_early.shape[0], wd_buf.shape[0]
    wd_copy = load(wd_ref.at[pl.ds(early, late)], wd_buf, sems.at[0])
    wu_copy = load(wu_ref.at[pl.ds(0, wu_out.shape[0])], wu_out, sems.at[1])
    at = 0
    for piece in pieces:
        top = jnp.max(jnp.abs(piece[...].astype(jnp.float32)), axis=1, keepdims=True)
        unit_ref[at : at + piece.shape[0], :] = 16.0 * jnp.maximum(top, 1e-30)
        at += piece.shape[0]
    gated = jnp.concatenate([piece[...] for piece in pieces], axis=0)
    for at in range(0, early + late, late):
        if at == early:
            wd_copy.wait()
        wd = wd_early[at : at + late, :] if at < early else wd_buf[...]
        du_ref[:, at : at + late] = (rows_t(gated, wd) * slope_ref[:, at : at + late]).astype(du_ref.dtype)
    wu_copy.wait()


def dh_kernel(du_ref, unit_ref, early_ref, wu_ref, *refs):
    outs, (w_buf, sems) = refs[:-2], refs[-2:]
    n, early, width = outs[0].shape[0], early_ref.shape[0], w_buf.shape[1]
    copies = load_parts(wu_ref, early, w_buf, sems)
    scale = 1.0 / unit_ref[...]
    for at in range(0, wu_ref.shape[0], width):
        if at < early:
            w = early_ref[at : at + width, :]
        else:
            k = (at - early) // width
            copies[k].wait()
            w = w_buf[k]
        dh = rows_t(du_ref[...], w) * scale
        for j, out in enumerate(outs):
            out[:, at : at + width] = dh[j * n : (j + 1) * n]


def finish_kernel(sum_ref, unit_ref, own_ref, rstd_ref, scale_ref, adjoint_ref, out_ref):
    normed = own_ref[...]
    scaled = (1.0 + scale_ref[...]) * (sum_ref[...] * unit_ref[: normed.shape[0], :])
    first = jnp.mean(scaled, axis=1, keepdims=True)
    second = jnp.mean(scaled * normed, axis=1, keepdims=True)
    d_latent = rstd_ref[...] * (scaled - first - normed * second)
    out_ref[...] = adjoint_ref[...].astype(jnp.float32) + step_scale * d_latent


def line_of_four(latent, adjoint, shift_row, scale_row, gate_row, b_up, w_up, w_down):
    rows, d = adjoint.shape
    tokens, ff = latent.shape[0], w_up.shape[1]
    me = lax.axis_index("fsdp")
    z = me >> 2
    is_mid = (z == 1) | (z == 2)
    f32, bf16 = jnp.float32, jnp.bfloat16
    work = 2 * tokens * d * ff
    shape = jax.ShapeDtypeStruct
    stay = lambda x: pltpu.with_memory_space_constraint(x, pltpu.HBM)
    w_up, w_down = stay(w_up), stay(w_down)
    scale = scale_row[None]

    b00 = (gate_row * adjoint.astype(f32)).astype(bf16)
    b30 = send(b00, CROSS)
    b10 = send(b00, PAIR)
    b01 = send(b00, SIDE)

    third, depth = ff // 3, d // 6
    u_shape = shape((tokens, ff), f32)
    w_scratch = [pltpu.VMEM((2, depth, ff), bf16)]
    w_sems = [pltpu.SemaphoreType.DMA((2,))]
    h, own_normed, own_rstd, u, wd_early = kernel(
        functools.partial(first_kernel, rows),
        [SMEM] + [HBM] * 5,
        [shape((tokens, d), bf16), shape((rows, d), f32), shape((rows, 1), f32), u_shape, shape((2 * third, d), bf16)],
        work // 2, 4 * d * third, 18,
        scratch_shapes=[pltpu.VMEM((tokens, d), bf16), pltpu.VMEM((1, d), f32), pltpu.VMEM((1, d), f32)]
        + w_scratch + [pltpu.SemaphoreType.DMA((3,))] + w_sems + [pltpu.SemaphoreType.DMA],
    )(me.reshape(1).astype(jnp.int32), stay(latent), stay(shift_row[None]), stay(scale), w_up, w_down)

    b10, b30 = after(b10, u), after(b30, u)
    m2 = send(b10, CROSS_MID)
    a2 = send(b30, PAIR)
    b11 = send(b10, SIDE)
    b31 = send(b30, SIDE)
    u = kernel(
        functools.partial(second_kernel, 2 * depth),
        [VMEM] * 2 + [HBM],
        u_shape,
        work // 3, 2 * d * third, 12,
        scratch_shapes=w_scratch + w_sems,
    )(h, after(u, b10, b30), w_up)

    b20 = after(jnp.where(is_mid, m2, a2), u)
    b21 = send(b20, SIDE)
    slope = kernel(
        functools.partial(third_kernel, 4 * depth),
        [VMEM] * 3 + [HBM],
        u_shape,
        work // 3, 2 * d * third, 12,
        scratch_shapes=w_scratch + w_sems,
    )(h, after(u, b20), b_up[None], w_up)

    cat = lambda *blocks: jnp.concatenate(blocks, axis=0)
    pieces = [cat(b00, b01, b10, b11), cat(b30, b31), cat(b20, b21)]
    pieces = pieces + [send(x, CORE) for x in pieces]
    early = 2 * depth
    du, unit, wu_early = kernel(
        du_kernel,
        [VMEM] * 8 + [HBM] * 2,
        [shape((tokens, ff), bf16), shape((tokens, 1), f32), shape((early, ff), bf16)],
        work, 2 * d * ff, 16,
        scratch_shapes=[pltpu.VMEM((third, d), bf16), pltpu.SemaphoreType.DMA((2,))],
    )(*pieces, wd_early, slope, w_down, w_up)
    quarters = kernel(
        dh_kernel,
        [VMEM] * 3 + [HBM],
        [shape((tokens // 4, d), f32)] * 4,
        work, 2 * d * ff, 20,
        scratch_shapes=[pltpu.VMEM((4, depth, ff), bf16), pltpu.SemaphoreType.DMA((4,))],
    )(du, unit, wu_early, w_up)
    return kernel(
        finish_kernel,
        [VMEM] * 6,
        shape((rows, d), f32),
        20 * rows * d, 10 * rows * d, 8,
    )(scatter_sums(quarters, is_mid, rows), unit, own_normed, own_rstd, scale, adjoint)


def solution(mesh):
    in_specs = (
        P("grp", None),
        P(("grp", "fsdp"), None),
        P("grp"),
        P("grp"),
        P("grp"),
        P("fsdp"),
        P(None, "fsdp"),
        P("fsdp", None),
    )
    out_specs = P(("grp", "fsdp"), None)
    body = line_of_four if mesh.shape["fsdp"] == 16 else general
    return jax.shard_map(body, mesh=mesh, in_specs=in_specs, out_specs=out_specs, check_vma=False)
```

```python
import functools
import jax
import jax.numpy as jnp
from jax import lax
from jax.experimental import pallas as pl
from jax.experimental.pallas import tpu as pltpu
from jax.sharding import PartitionSpec as P

step_scale = 0.5


def gelu_slope(u):
    k = 0.7978845608
    t = jnp.tanh(k * (u + 0.044715 * u * u * u))
    return 0.5 * (1.0 + t) + 0.5 * u * (1.0 - t * t) * k * (1.0 + 3.0 * 0.044715 * u * u)


def normalize(latent):
    values = latent.astype(jnp.float32)
    mean = jnp.mean(values, axis=1, keepdims=True)
    centred = values - mean
    rstd = lax.rsqrt(jnp.mean(centred * centred, axis=1, keepdims=True) + 1e-06)
    return (centred * rstd, rstd)


def finish(latent_rows, adjoint, scale_row, d_hidden):
    normed, rstd = normalize(latent_rows)
    scaled = (1.0 + scale_row) * d_hidden
    first = jnp.mean(scaled, axis=1, keepdims=True)
    second = jnp.mean(scaled * normed, axis=1, keepdims=True)
    d_latent = rstd * (scaled - first - normed * second)
    return adjoint.astype(jnp.float32) + step_scale * d_latent


def rows_t(a, b):
    return lax.dot_general(a, b, (((1,), (1,)), ((), ())), preferred_element_type=jnp.float32)


def general(latent, adjoint, shift_row, scale_row, gate_row, b_up, w_up, w_down):
    own_rows = adjoint.shape[0]
    start = lax.axis_index("fsdp") * own_rows
    normed, _ = normalize(latent)
    hidden_in = (normed * (1.0 + scale_row) + shift_row).astype(jnp.bfloat16)
    gated = (gate_row * adjoint.astype(jnp.float32)).astype(jnp.bfloat16)
    gated = lax.all_gather(gated, "fsdp", axis=0, tiled=True)
    upper = jnp.dot(hidden_in, w_up, preferred_element_type=jnp.float32) + b_up.astype(jnp.float32)
    d_upper = (rows_t(gated, w_down) * gelu_slope(upper)).astype(jnp.bfloat16)
    d_hidden = lax.psum_scatter(rows_t(d_upper, w_up), "fsdp", scatter_dimension=0, tiled=True)
    return finish(lax.dynamic_slice_in_dim(latent, start, own_rows, 0), adjoint, scale_row, d_hidden)


CORE = [(i, i ^ 1) for i in range(16)]
SIDE = [(i, i ^ 2) for i in range(16)]
PAIR = [(i, i ^ 4) for i in range(16)]
CROSS = [(i, i ^ 12) for i in range(16)]


def send(x, pairs):
    return lax.ppermute(x, "fsdp", pairs)


def half(x):
    return x.astype(jnp.float16)


def wide(x):
    return x.astype(jnp.float32)


def after(x, *done):
    return lax.optimization_barrier((x, *done))[0]


def scatter_sums(chunks, rows):
    cut = lambda x, k: x[k * rows : (k + 1) * rows]
    sums = []
    for near_early, near_late, far_early, far_late in chunks:
        c_late = send(half(far_late), CORE)
        c_early = send(half(far_early), CORE)
        late = near_late + wide(c_late)
        early = near_early + wide(c_early)
        p00, p01, p10, p11 = [cut(early, k) for k in range(4)]
        p30, p31, p20, p21 = [cut(late, k) for k in range(4)]
        z21 = send(half(p21), PAIR)
        y1 = send(half(p11), SIDE)
        y3 = send(half(p31 + wide(z21)), SIDE)
        z20 = send(half(p20), PAIR)
        z3 = send(half(p30 + wide(y3) + wide(z20)), CROSS)
        z1 = send(after(half(p10 + wide(y1)), z20), PAIR)
        y0 = send(after(half(p01), y3), SIDE)
        sums.append(p00 + wide(y0) + wide(z1) + wide(z3))
    return sums


VMEM = pl.BlockSpec(memory_space=pltpu.VMEM)
SMEM = pl.BlockSpec(memory_space=pltpu.SMEM)
HBM = pl.BlockSpec(memory_space=pltpu.HBM)


def kernel(body, specs, out_shape, flops, moved, grant, **more):
    several = isinstance(out_shape, (list, tuple))
    return pl.pallas_call(
        body,
        in_specs=specs,
        out_specs=[VMEM] * len(out_shape) if several else VMEM,
        out_shape=out_shape,
        compiler_params=pltpu.CompilerParams(vmem_limit_bytes=grant * 2**20),
        cost_estimate=pl.CostEstimate(flops=flops, bytes_accessed=moved, transcendentals=0),
        **more,
    )


def load(source, target, sem):
    copy = pltpu.make_async_copy(source, target, sem)
    copy.start()
    return copy


def load_parts(source, start, buf, sems):
    n = buf.shape[1]
    return [load(source.at[pl.ds(start + k * n, n)], buf.at[k], sems.at[k]) for k in range(buf.shape[0])]


def normalize_rows(rows, me_ref, latent_ref, shift_ref, scale_ref, h_ref, own_ref, rstd_ref):
    def block(p):
        g = (p >> 1) & 3
        owner = me_ref[0] ^ ((p >> 3) | ((p & 1) << 1) | ((g ^ (g >> 1)) << 2))
        values = latent_ref[pl.ds(pl.multiple_of(owner * rows, rows), rows), :].astype(jnp.float32)
        mean = jnp.mean(values, axis=1, keepdims=True)
        centred = values - mean
        rstd = lax.rsqrt(jnp.mean(centred * centred, axis=1, keepdims=True) + 1e-06)
        normed = centred * rstd
        h = normed * (1.0 + scale_ref[...]) + shift_ref[...]
        h_ref[pl.ds(pl.multiple_of(p * rows, rows), rows), :] = h.astype(h_ref.dtype)
        return normed, rstd

    own_ref[...], rstd_ref[...] = block(0)

    def step(p, _):
        block(p)
        return 0

    lax.fori_loop(1, 16, step, 0, unroll=3)


def add_product(acc, at, h_ref, w):
    product = jnp.dot(h_ref[:, at : at + w.shape[0]], w, preferred_element_type=jnp.float32)
    return product if acc is None else acc + product


def first_kernel(rows, me_ref, latent_ref, shift_ref, scale_ref, wu_ref, wd_ref, h_ref, own_ref, rstd_ref, u_ref, next_ref, wd_out, latent_buf, shift_buf, scale_buf, w_buf, sems, w_sems, out_sems):
    copies = [
        load(source, target, sems.at[k])
        for k, (source, target) in enumerate([(latent_ref, latent_buf), (shift_ref, shift_buf), (scale_ref, scale_buf)])
    ]
    n = w_buf.shape[1]
    w_copies = load_parts(wu_ref, 0, w_buf, w_sems)
    outs = [
        load(wu_ref.at[pl.ds(2 * n, n)], next_ref, out_sems.at[0]),
        load(wd_ref.at[pl.ds(0, wd_out.shape[0])], wd_out, out_sems.at[1]),
    ]
    for copy in copies:
        copy.wait()
    normalize_rows(rows, me_ref, latent_buf, shift_buf, scale_buf, h_ref, own_ref, rstd_ref)
    u = None
    for k, copy in enumerate(w_copies):
        copy.wait()
        u = add_product(u, k * n, h_ref, w_buf[k])
    u_ref[...] = u
    for copy in outs:
        copy.wait()


def second_kernel(start, h_ref, u_ref, w_ref, wu_ref, u_out, next_ref, w_buf, sems):
    n = w_buf.shape[0]
    copy = load(wu_ref.at[pl.ds(start + n, n)], w_buf, sems.at[0])
    ahead = load(wu_ref.at[pl.ds(start + 2 * n, n)], next_ref, sems.at[1])
    u = add_product(u_ref[...], start, h_ref, w_ref[...])
    copy.wait()
    u_out[...] = add_product(u, start + n, h_ref, w_buf[...])
    ahead.wait()


def third_kernel(start, h_ref, u_ref, w_ref, b_ref, wu_ref, wd_ref, slope_out, wd_out, w_buf, sems):
    n = w_buf.shape[0]
    copy = load(wu_ref.at[pl.ds(start + n, n)], w_buf, sems.at[0])
    ahead = load(wd_ref.at[pl.ds(wd_out.shape[0], wd_out.shape[0])], wd_out, sems.at[1])
    u = add_product(u_ref[...], start, h_ref, w_ref[...])
    copy.wait()
    slope_out[...] = add_product(u, start + n, h_ref, w_buf[...])
    width = slope_out.shape[1] // 3
    for j in range(3):
        cut = slice(j * width, (j + 1) * width)
        slope_out[:, cut] = gelu_slope(slope_out[:, cut] + b_ref[:, cut].astype(jnp.float32))
    ahead.wait()


def du_kernel(*refs):
    pieces, (wd0_ref, wd1_ref, slope_ref, wd_ref, wu_ref, du_ref, unit_ref, wu_out, wd_buf, sems) = refs[:6], refs[6:]
    width, at = wd_buf.shape[0], 0
    wd_copy = load(wd_ref.at[pl.ds(2 * width, width)], wd_buf, sems.at[0])
    wu_copy = load(wu_ref.at[pl.ds(0, wu_out.shape[0])], wu_out, sems.at[1])
    for piece in pieces:
        top = jnp.max(jnp.abs(piece[...].astype(jnp.float32)), axis=1, keepdims=True)
        unit_ref[at : at + piece.shape[0], :] = 16.0 * jnp.maximum(top, 1e-30)
        at += piece.shape[0]
    gated = jnp.concatenate([piece[...] for piece in pieces], axis=0)
    for k, wd in enumerate((wd0_ref, wd1_ref, wd_buf)):
        if k == 2:
            wd_copy.wait()
        cut = slice(k * width, (k + 1) * width)
        du_ref[:, cut] = (rows_t(gated, wd[...]) * slope_ref[:, cut]).astype(du_ref.dtype)
    wu_copy.wait()


def dh_kernel(start, ahead, du_ref, unit_ref, early_ref, wu_ref, *refs):
    outs, refs = refs[:4], refs[4:]
    if ahead:
        ahead_out, w_buf, sems, ahead_sem = refs
    else:
        w_buf, sems = refs
    n, early, width = outs[0].shape[0], early_ref.shape[0], w_buf.shape[1]
    copies = load_parts(wu_ref, start + early, w_buf, sems)
    if ahead:
        ahead_copy = load(wu_ref.at[pl.ds(start + outs[0].shape[1], ahead)], ahead_out, ahead_sem)
    scale = 1.0 / unit_ref[...]
    for at in range(0, outs[0].shape[1], width):
        if at < early:
            w = early_ref[at : at + width, :]
        else:
            k = (at - early) // width
            copies[k].wait()
            w = w_buf[k]
        dh = rows_t(du_ref[...], w) * scale
        for j, out in enumerate(outs):
            out[:, at : at + width] = dh[j * n : (j + 1) * n]
    if ahead:
        ahead_copy.wait()


def finish_kernel(sum_ref, unit_ref, own_ref, rstd_ref, scale_ref, adjoint_ref, out_ref):
    normed = own_ref[...]
    scaled = (1.0 + scale_ref[...]) * (sum_ref[...] * unit_ref[: normed.shape[0], :])
    first = jnp.mean(scaled, axis=1, keepdims=True)
    second = jnp.mean(scaled * normed, axis=1, keepdims=True)
    d_latent = rstd_ref[...] * (scaled - first - normed * second)
    out_ref[...] = adjoint_ref[...].astype(jnp.float32) + step_scale * d_latent


def line_of_four(latent, adjoint, shift_row, scale_row, gate_row, b_up, w_up, w_down):
    rows, d = adjoint.shape
    tokens, ff = latent.shape[0], w_up.shape[1]
    me = lax.axis_index("fsdp")
    f32, bf16 = jnp.float32, jnp.bfloat16
    work = 2 * tokens * d * ff
    shape = jax.ShapeDtypeStruct
    stay = lambda x: pltpu.with_memory_space_constraint(x, pltpu.HBM)
    w_up, w_down = stay(w_up), stay(w_down)
    scale = scale_row[None]

    b00 = (gate_row * adjoint.astype(f32)).astype(bf16)
    b30 = send(b00, CROSS)
    b10 = send(b00, PAIR)
    b01 = send(b00, SIDE)

    depth, third = d // 6, ff // 3
    wd_shape = shape((third, d), bf16)
    u_shape, part_shape = shape((tokens, ff), f32), shape((depth, ff), bf16)
    part = pltpu.VMEM((depth, ff), bf16)
    sems = lambda n: pltpu.SemaphoreType.DMA((n,))
    h, own_normed, own_rstd, u, part2, wd0 = kernel(
        functools.partial(first_kernel, rows),
        [SMEM] + [HBM] * 5,
        [shape((tokens, d), bf16), shape((rows, d), f32), shape((rows, 1), f32), u_shape, part_shape, wd_shape],
        work // 2, 2 * d * ff, 18,
        scratch_shapes=[pltpu.VMEM((tokens, d), bf16), pltpu.VMEM((1, d), f32), pltpu.VMEM((1, d), f32)]
        + [pltpu.VMEM((2, depth, ff), bf16), sems(3), sems(2), sems(2)],
    )(me.reshape(1).astype(jnp.int32), stay(latent), stay(shift_row[None]), stay(scale), w_up, w_down)

    b10, b30 = after(b10, u), after(b30, u)
    b31 = send(b30, SIDE)
    b20 = send(b30, PAIR)
    u, part4 = kernel(
        functools.partial(second_kernel, 2 * depth),
        [VMEM] * 3 + [HBM],
        [u_shape, part_shape],
        work // 3, d * ff, 12,
        scratch_shapes=[part, sems(2)],
    )(h, after(u, b30), part2, w_up)

    b31 = after(b31, u)
    b21 = send(b31, PAIR)
    b11 = send(after(b10, b31), SIDE)
    slope, wd1 = kernel(
        functools.partial(third_kernel, 4 * depth),
        [VMEM] * 4 + [HBM] * 2,
        [u_shape, wd_shape],
        work // 3, d * ff, 12,
        scratch_shapes=[part, sems(2)],
    )(h, after(u, b31), part4, b_up[None], w_up, w_down)

    b11, b21 = after(b11, slope), after(b21, slope)
    cat = lambda *blocks: jnp.concatenate(blocks, axis=0)
    c0, c13, c32 = [send(cat(*x), CORE) for x in ((b00, b01), (b10, b30), (b31, b20))]
    c11, c21 = send(b11, CORE), send(b21, CORE)
    pieces = [cat(b00, b01, b10, b11), cat(b30, b31), cat(b20, b21)]
    pieces += [cat(c0, c13[:rows], c11), cat(c13[rows:], c32[:rows]), cat(c32[rows:], c21)]
    early = 2 * depth
    du, unit, wu_early = kernel(
        du_kernel,
        [VMEM] * 9 + [HBM] * 2,
        [shape((tokens, ff), bf16), shape((tokens, 1), f32), shape((early, ff), bf16)],
        work, 2 * d * ff, 16,
        scratch_shapes=[pltpu.VMEM((third, d), bf16), sems(2)],
    )(*pieces, wd0, wd1, slope, w_down, w_up)
    quarters = kernel(
        functools.partial(dh_kernel, 0, 0),
        [VMEM] * 3 + [HBM],
        [shape((tokens // 4, d), f32)] * 4,
        work, 2 * d * ff, 20,
        scratch_shapes=[pltpu.VMEM((4, depth, ff), bf16), pltpu.SemaphoreType.DMA((4,))],
    )(du, unit, wu_early, w_up)
    (total,) = scatter_sums([quarters], rows)
    return kernel(
        finish_kernel,
        [VMEM] * 6,
        shape((rows, d), f32),
        20 * rows * d, 10 * rows * d, 8,
    )(total, unit, own_normed, own_rstd, scale, adjoint)


def solution(mesh):
    in_specs = (
        P("grp", None),
        P(("grp", "fsdp"), None),
        P("grp"),
        P("grp"),
        P("grp"),
        P("fsdp"),
        P(None, "fsdp"),
        P("fsdp", None),
    )
    out_specs = P(("grp", "fsdp"), None)
    body = line_of_four if mesh.shape["fsdp"] == 16 else general
    return jax.shard_map(body, mesh=mesh, in_specs=in_specs, out_specs=out_specs, check_vma=False)
```

```python
import functools
import jax
import jax.numpy as jnp
from jax import lax
from jax.experimental import pallas as pl
from jax.experimental.pallas import tpu as pltpu
from jax.sharding import PartitionSpec as P

step_scale = 0.5


def gelu_slope(u):
    k = 0.7978845608
    t = jnp.tanh(k * (u + 0.044715 * u * u * u))
    return 0.5 * (1.0 + t) + 0.5 * u * (1.0 - t * t) * k * (1.0 + 3.0 * 0.044715 * u * u)


def normalize(latent):
    values = latent.astype(jnp.float32)
    mean = jnp.mean(values, axis=1, keepdims=True)
    centred = values - mean
    rstd = lax.rsqrt(jnp.mean(centred * centred, axis=1, keepdims=True) + 1e-06)
    return (centred * rstd, rstd)


def finish(latent_rows, adjoint, scale_row, d_hidden):
    normed, rstd = normalize(latent_rows)
    scaled = (1.0 + scale_row) * d_hidden
    first = jnp.mean(scaled, axis=1, keepdims=True)
    second = jnp.mean(scaled * normed, axis=1, keepdims=True)
    d_latent = rstd * (scaled - first - normed * second)
    return adjoint.astype(jnp.float32) + step_scale * d_latent


def rows_t(a, b):
    return lax.dot_general(a, b, (((1,), (1,)), ((), ())), preferred_element_type=jnp.float32)


def general(latent, adjoint, shift_row, scale_row, gate_row, b_up, w_up, w_down):
    own_rows = adjoint.shape[0]
    start = lax.axis_index("fsdp") * own_rows
    normed, _ = normalize(latent)
    hidden_in = (normed * (1.0 + scale_row) + shift_row).astype(jnp.bfloat16)
    gated = (gate_row * adjoint.astype(jnp.float32)).astype(jnp.bfloat16)
    gated = lax.all_gather(gated, "fsdp", axis=0, tiled=True)
    upper = jnp.dot(hidden_in, w_up, preferred_element_type=jnp.float32) + b_up.astype(jnp.float32)
    d_upper = (rows_t(gated, w_down) * gelu_slope(upper)).astype(jnp.bfloat16)
    d_hidden = lax.psum_scatter(rows_t(d_upper, w_up), "fsdp", scatter_dimension=0, tiled=True)
    return finish(lax.dynamic_slice_in_dim(latent, start, own_rows, 0), adjoint, scale_row, d_hidden)


CORE = [(i, i ^ 1) for i in range(16)]
SIDE = [(i, i ^ 2) for i in range(16)]
PAIR = [(i, i ^ 4) for i in range(16)]
CROSS = [(i, i ^ 12) for i in range(16)]


def send(x, pairs):
    return lax.ppermute(x, "fsdp", pairs)


def half(x):
    return x.astype(jnp.float16)


def wide(x):
    return x.astype(jnp.float32)


def after(x, *done):
    return lax.optimization_barrier((x, *done))[0]


def scatter_sums(chunks, rows):
    cut = lambda x, k: x[k * rows : (k + 1) * rows]
    sums = []
    for near_early, near_late, far_early, far_late in chunks:
        c_late = send(half(far_late), CORE)
        c_early = send(half(far_early), CORE)
        late = near_late + wide(c_late)
        early = near_early + wide(c_early)
        p00, p01, p10, p11 = [cut(early, k) for k in range(4)]
        p30, p31, p20, p21 = [cut(late, k) for k in range(4)]
        z21 = send(half(p21), PAIR)
        y1 = send(half(p11), SIDE)
        y3 = send(half(p31 + wide(z21)), SIDE)
        z20 = send(half(p20), PAIR)
        z3 = send(half(p30 + wide(y3) + wide(z20)), CROSS)
        z1 = send(after(half(p10 + wide(y1)), z21), PAIR)
        y0 = send(after(half(p01), y3), SIDE)
        sums.append(p00 + wide(y0) + wide(z1) + wide(z3))
    return sums


VMEM = pl.BlockSpec(memory_space=pltpu.VMEM)
SMEM = pl.BlockSpec(memory_space=pltpu.SMEM)
HBM = pl.BlockSpec(memory_space=pltpu.HBM)


def kernel(body, specs, out_shape, flops, moved, grant, **more):
    several = isinstance(out_shape, (list, tuple))
    return pl.pallas_call(
        body,
        in_specs=specs,
        out_specs=[VMEM] * len(out_shape) if several else VMEM,
        out_shape=out_shape,
        compiler_params=pltpu.CompilerParams(vmem_limit_bytes=grant * 2**20),
        cost_estimate=pl.CostEstimate(flops=flops, bytes_accessed=moved, transcendentals=0),
        **more,
    )


def load(source, target, sem):
    copy = pltpu.make_async_copy(source, target, sem)
    copy.start()
    return copy


def load_parts(source, start, buf, sems):
    n = buf.shape[1]
    return [load(source.at[pl.ds(start + k * n, n)], buf.at[k], sems.at[k]) for k in range(buf.shape[0])]


def normalize_rows(rows, me_ref, latent_ref, shift_ref, scale_ref, h_ref, own_ref, rstd_ref):
    def block(p):
        g = (p >> 1) & 3
        owner = me_ref[0] ^ ((p >> 3) | ((p & 1) << 1) | ((g ^ (g >> 1)) << 2))
        values = latent_ref[pl.ds(pl.multiple_of(owner * rows, rows), rows), :].astype(jnp.float32)
        mean = jnp.mean(values, axis=1, keepdims=True)
        centred = values - mean
        rstd = lax.rsqrt(jnp.mean(centred * centred, axis=1, keepdims=True) + 1e-06)
        normed = centred * rstd
        h = normed * (1.0 + scale_ref[...]) + shift_ref[...]
        h_ref[pl.ds(pl.multiple_of(p * rows, rows), rows), :] = h.astype(h_ref.dtype)
        return normed, rstd

    own_ref[...], rstd_ref[...] = block(0)

    def step(p, _):
        block(p)
        return 0

    lax.fori_loop(1, 16, step, 0, unroll=3)


def add_product(acc, at, h_ref, w):
    product = jnp.dot(h_ref[:, at : at + w.shape[0]], w, preferred_element_type=jnp.float32)
    return product if acc is None else acc + product


def first_kernel(rows, me_ref, latent_ref, shift_ref, scale_ref, wu_ref, wd_ref, h_ref, own_ref, rstd_ref, wu_out, wd_out, latent_buf, shift_buf, scale_buf, sems, out_sems):
    copies = [
        load(source, target, sems.at[k])
        for k, (source, target) in enumerate([(latent_ref, latent_buf), (shift_ref, shift_buf), (scale_ref, scale_buf)])
    ]
    outs = [
        load(source.at[pl.ds(0, out.shape[0])], out, out_sems.at[k])
        for k, (source, out) in enumerate([(wu_ref, wu_out), (wd_ref, wd_out)])
    ]
    for copy in copies:
        copy.wait()
    normalize_rows(rows, me_ref, latent_buf, shift_buf, scale_buf, h_ref, own_ref, rstd_ref)
    for copy in outs:
        copy.wait()


def second_kernel(h_ref, w_ref, wu_ref, wd_ref, u_out, next_ref, wd_out, w_buf, sems):
    early, n = w_ref.shape[0], w_buf.shape[0]
    copy = load(wu_ref.at[pl.ds(early, n)], w_buf, sems.at[0])
    ahead = load(wu_ref.at[pl.ds(early + n, n)], next_ref, sems.at[1])
    wd_copy = load(wd_ref.at[pl.ds(wd_out.shape[0], wd_out.shape[0])], wd_out, sems.at[2])
    u = add_product(None, 0, h_ref, w_ref[...])
    copy.wait()
    u_out[...] = add_product(u, early, h_ref, w_buf[...])
    ahead.wait()
    wd_copy.wait()


def third_kernel(h_ref, u_ref, w_ref, b_ref, wu_ref, wd_ref, slope_out, wd_out, w_buf, w_sems, wd_sem):
    parts, n, _ = w_buf.shape
    start = wu_ref.shape[0] - parts * n
    copies = load_parts(wu_ref, start, w_buf, w_sems)
    ahead = load(wd_ref.at[pl.ds(2 * wd_out.shape[0], wd_out.shape[0])], wd_out, wd_sem)
    u = add_product(u_ref[...], start - n, h_ref, w_ref[...])
    for k, copy in enumerate(copies):
        copy.wait()
        u = add_product(u, start + k * n, h_ref, w_buf[k])
    slope_out[...] = u
    width = slope_out.shape[1] // 3
    for j in range(3):
        cut = slice(j * width, (j + 1) * width)
        slope_out[:, cut] = gelu_slope(slope_out[:, cut] + b_ref[:, cut].astype(jnp.float32))
    ahead.wait()


def du_kernel(*refs):
    pieces, wds, (slope_ref, wu_ref, du_ref, unit_ref, wu_out, sem) = refs[:6], refs[6:9], refs[9:]
    wu_copy = load(wu_ref.at[pl.ds(0, wu_out.shape[0])], wu_out, sem)
    at = 0
    for piece in pieces:
        top = jnp.max(jnp.abs(piece[...].astype(jnp.float32)), axis=1, keepdims=True)
        unit_ref[at : at + piece.shape[0], :] = 16.0 * jnp.maximum(top, 1e-30)
        at += piece.shape[0]
    gated = jnp.concatenate([piece[...] for piece in pieces], axis=0)
    for k, wd in enumerate(wds):
        cut = slice(k * wd.shape[0], (k + 1) * wd.shape[0])
        du_ref[:, cut] = (rows_t(gated, wd[...]) * slope_ref[:, cut]).astype(du_ref.dtype)
    wu_copy.wait()


def dh_kernel(width, du_ref, unit_ref, early_ref, wu_ref, *refs):
    outs, (w_buf, sem) = refs[:-2], refs[-2:]
    n, early = outs[0].shape[0], early_ref.shape[0]
    copy = load(wu_ref.at[pl.ds(early, w_buf.shape[0])], w_buf, sem)
    scale = 1.0 / unit_ref[...]
    for at in range(0, wu_ref.shape[0], width):
        if at == early:
            copy.wait()
        w = early_ref[at : at + width, :] if at < early else w_buf[at - early : at - early + width, :]
        dh = rows_t(du_ref[...], w) * scale
        for j, out in enumerate(outs):
            out[:, at : at + width] = dh[j * n : (j + 1) * n]


def finish_kernel(sum_ref, unit_ref, own_ref, rstd_ref, scale_ref, adjoint_ref, out_ref):
    normed = own_ref[...]
    scaled = (1.0 + scale_ref[...]) * (sum_ref[...] * unit_ref[: normed.shape[0], :])
    first = jnp.mean(scaled, axis=1, keepdims=True)
    second = jnp.mean(scaled * normed, axis=1, keepdims=True)
    d_latent = rstd_ref[...] * (scaled - first - normed * second)
    out_ref[...] = adjoint_ref[...].astype(jnp.float32) + step_scale * d_latent


def line_of_four(latent, adjoint, shift_row, scale_row, gate_row, b_up, w_up, w_down):
    rows, d = adjoint.shape
    tokens, ff = latent.shape[0], w_up.shape[1]
    me = lax.axis_index("fsdp")
    f32, bf16 = jnp.float32, jnp.bfloat16
    work = 2 * tokens * d * ff
    shape = jax.ShapeDtypeStruct
    stay = lambda x: pltpu.with_memory_space_constraint(x, pltpu.HBM)
    w_up, w_down = stay(w_up), stay(w_down)
    scale = scale_row[None]

    b00 = (gate_row * adjoint.astype(f32)).astype(bf16)
    b30 = send(b00, CROSS)
    b10 = send(b00, PAIR)
    b01 = send(b00, SIDE)

    depth, third = d // 6, ff // 3
    wd_shape = shape((third, d), bf16)
    u_shape, part_shape = shape((tokens, ff), f32), shape((depth, ff), bf16)
    sems = lambda n: pltpu.SemaphoreType.DMA((n,))
    h, own_normed, own_rstd, wu_early, wd0 = kernel(
        functools.partial(first_kernel, rows),
        [SMEM] + [HBM] * 5,
        [shape((tokens, d), bf16), shape((rows, d), f32), shape((rows, 1), f32), shape((2 * depth, ff), bf16), wd_shape],
        work // 2, 2 * d * ff, 16,
        scratch_shapes=[pltpu.VMEM((tokens, d), bf16), pltpu.VMEM((1, d), f32), pltpu.VMEM((1, d), f32), sems(3), sems(2)],
    )(me.reshape(1).astype(jnp.int32), stay(latent), stay(shift_row[None]), stay(scale), w_up, w_down)

    cat = lambda *blocks: jnp.concatenate(blocks, axis=0)
    b01, b30, b10, _ = lax.optimization_barrier((b01, b30, b10, h))
    b31 = send(b30, SIDE)
    b20 = send(b30, PAIR)
    c0, c13 = send(cat(b00, b01), CORE), send(cat(b10, b30), CORE)
    u, part, wd1 = kernel(
        second_kernel,
        [VMEM] * 2 + [HBM] * 2,
        [u_shape, part_shape, wd_shape],
        work // 3, d * ff, 12,
        scratch_shapes=[pltpu.VMEM((depth, ff), bf16), sems(3)],
    )(after(h, b30), wu_early, w_up, w_down)

    b31 = after(b31, u)
    b21 = send(b31, PAIR)
    b11 = send(after(b10, b31), SIDE)
    c32 = send(cat(b31, b20), CORE)
    slope, wd2 = kernel(
        third_kernel,
        [VMEM] * 4 + [HBM] * 2,
        [u_shape, wd_shape],
        work // 3, d * ff, 12,
        scratch_shapes=[pltpu.VMEM((2, depth, ff), bf16), sems(2), pltpu.SemaphoreType.DMA],
    )(h, after(u, b31, b20, c0, c13), part, b_up[None], w_up, w_down)

    b11, b21 = after(b11, slope), after(b21, slope)
    c11, c21 = send(b11, CORE), send(b21, CORE)
    pieces = [cat(b00, b01, b10, b11), cat(b30, b31), cat(b20, b21)]
    pieces += [cat(c0, c13[:rows], c11), cat(c13[rows:], c32[:rows]), cat(c32[rows:], c21)]
    early = 4 * depth
    du, unit, wu_early = kernel(
        du_kernel,
        [VMEM] * 10 + [HBM],
        [shape((tokens, ff), bf16), shape((tokens, 1), f32), shape((early, ff), bf16)],
        work, 2 * d * ff, 10,
        scratch_shapes=[pltpu.SemaphoreType.DMA],
    )(*pieces, wd0, wd1, wd2, slope, w_up)
    quarters = kernel(
        functools.partial(dh_kernel, depth),
        [VMEM] * 3 + [HBM],
        [shape((tokens // 4, d), f32)] * 4,
        work, 2 * d * ff, 12,
        scratch_shapes=[pltpu.VMEM((2 * depth, ff), bf16), pltpu.SemaphoreType.DMA],
    )(du, unit, wu_early, w_up)
    (total,) = scatter_sums([quarters], rows)
    return kernel(
        finish_kernel,
        [VMEM] * 6,
        shape((rows, d), f32),
        20 * rows * d, 10 * rows * d, 8,
    )(total, unit, own_normed, own_rstd, scale, adjoint)


def solution(mesh):
    in_specs = (
        P("grp", None),
        P(("grp", "fsdp"), None),
        P("grp"),
        P("grp"),
        P("grp"),
        P("fsdp"),
        P(None, "fsdp"),
        P("fsdp", None),
    )
    out_specs = P(("grp", "fsdp"), None)
    body = line_of_four if mesh.shape["fsdp"] == 16 else general
    return jax.shard_map(body, mesh=mesh, in_specs=in_specs, out_specs=out_specs, check_vma=False)
```
